256 devices in a mesh: blk: 256 (over y, z, x, core).
Axes of the slice: x: 4, y: 4, z: 8, core: 2. Of those that a mesh axis runs over, the one named last changes fastest.
Arguments:
- gradients: bfloat16 [131072, 2048], P('blk')
- partner: int32 [256], P('blk'), may hold values from 0 to 255, as said below
- cover: float32 [131072], P('blk'), may hold values from -0.1 to 0.4
Outputs:
- cross_tile: float32 [131072, 512], P('blk')
- self_tile: float32 [131072, 512], P('blk')
- gains: float32 [131072], P('blk')
The draws below stay inside these ranges and needn't reach their ends.
Inputs may be any that keep to these rules, and one draw needn't show every extreme that they name: partner[b] = b XOR m for one m of 1 to 255, the same for all blocks.
All inputs are finite; a program needn't handle non-finite values.
Results may differ from the reference program's by a relative error of at most 0.00077.
Values may be sent and summed in bfloat16 or wider, within the bound.
A program may use at most 64 MiB of HBM per device.

```python
import jax
import jax.numpy as jnp
from jax import lax

G = 2048
ROWS = 512
EXAMPLES = 131072
N_BLK = 256


def draw_gradients(key, part):
    key = jax.random.fold_in(key, 11)
    k_center, k_noise, k_scale = jax.random.split(key, 3)
    centers = jax.random.normal(k_center, (8, G), jnp.float32)
    labels = jnp.arange(EXAMPLES, dtype=jnp.int32) % 8
    noise = jax.random.normal(k_noise, (EXAMPLES, G), jnp.float32)
    scale = jnp.exp(jax.random.uniform(k_scale, (EXAMPLES, 1), jnp.float32, 0.0, 2.4))
    return (scale * (noise + 0.8 * centers[labels])).astype(jnp.bfloat16)


def draw_partner(key, part):
    key = jax.random.fold_in(key, 23)
    flip = jax.random.randint(key, (), 1, N_BLK, jnp.int32)
    return jnp.bitwise_xor(jnp.arange(N_BLK, dtype=jnp.int32), flip)


def block_scale(rng, dims, cuts, smallest, high):
    factor_of = 1.0
    for axis_at, shards_of in cuts:
        steps = jax.random.uniform(jax.random.fold_in(jax.random.fold_in(rng, 6), axis_at), (shards_of,), jnp.float32, smallest / len(cuts), high / len(cuts))
        factor_of = factor_of * jnp.repeat(jnp.exp(steps), dims[axis_at] // shards_of).reshape((-1,) + (1,) * (len(dims) - 1 - axis_at))
    return factor_of


def setup_inputs(seed: int = 0) -> dict:
    streams_of = jax.random.split(jax.random.key(seed), 4)
    return {
        "gradients": draw_gradients(jax.random.fold_in(streams_of[3], 71), 0),
        "partner": draw_partner(jax.random.fold_in(streams_of[3], 71), 0),
        "cover": jnp.clip(-0.1 + 0.5 * jax.random.uniform(streams_of[2], (EXAMPLES,), jnp.float32) ** block_scale(streams_of[2], (EXAMPLES,), ((0, 256),), -0.2, 0.2), -0.1, 0.4),
    }


def reference(gradients, partner, cover):
    values = gradients.astype(jnp.float32)
    scale = 1.0 / jnp.sqrt(lax.optimization_barrier(jnp.sum(values * values, axis=1, keepdims=True)) + 1e-06)
    unit = (values * scale).astype(jnp.bfloat16)
    blocks = unit.reshape(N_BLK, ROWS, G)
    covers = cover.reshape(N_BLK, ROWS)

    def one_block(index):
        mine = blocks[index]
        other = blocks[partner[index]]
        cross = lax.dot_general(mine, other, (((1,), (1,)), ((), ())), preferred_element_type=jnp.float32)
        own = lax.dot_general(mine, mine, (((1,), (1,)), ((), ())), preferred_element_type=jnp.float32)
        gain = lax.optimization_barrier(jnp.sum(jnp.maximum(cross - covers[index][:, None], 0.0), axis=0))
        return (cross, own, gain)
    cross, own, gain = lax.map(one_block, jnp.arange(N_BLK, dtype=jnp.int32))
    return (cross.reshape(EXAMPLES, ROWS), own.reshape(EXAMPLES, ROWS), gain.reshape(EXAMPLES))
```

```python
import jax
import jax.numpy as jnp
from jax import lax
from jax.sharding import PartitionSpec as P


def product(left, right):
    return lax.dot_general(
        left, right, (((1,), (1,)), ((), ())), preferred_element_type=jnp.float32
    )


def shards(gradients, partner, cover):
    n = lax.axis_size("blk")
    myself = lax.axis_index("blk")
    flip = jnp.bitwise_xor(partner[0], myself)
    values = gradients.astype(jnp.float32)
    scale = 1.0 / jnp.sqrt(jnp.sum(values * values, axis=1, keepdims=True) + 1e-06)
    unit = (values * scale).astype(jnp.bfloat16)

    def exchange(m):
        return lambda block: lax.ppermute(block, "blk", [(i, i ^ m) for i in range(n)])

    other = lax.switch(flip - 1, [exchange(m) for m in range(1, n)], unit)
    own = product(unit, unit)
    cross = product(unit, other)
    gain = jnp.sum(jnp.maximum(cross - cover[:, None], 0.0), axis=0)
    return (cross, own, gain)


def solution(mesh):
    placed = (P("blk", None), P("blk"), P("blk"))
    return jax.shard_map(
        shards,
        mesh=mesh,
        in_specs=placed,
        out_specs=(P("blk", None), P("blk", None), P("blk")),
        check_vma=False,
    )
```

```python
import functools

import jax
import jax.numpy as jnp
from jax import lax
from jax.experimental import pallas as pl
from jax.experimental.pallas import tpu as pltpu
from jax.sharding import PartitionSpec as P

ROWS = 512
G = 2048
STEP = 128
PARTS = ROWS // STEP
MESH = pl.DeviceIdType.MESH


def bit_of(index, k):
    return lax.rem(lax.div(index, 1 << k), 2)


def partner_of(me, flip):
    other = me
    for k in range(8):
        if flip >> k & 1:
            other = other + (1 << k) * (1 - 2 * bit_of(me, k))
    return other


def gives_of(me, flip):
    core = bit_of(me, 0)
    if flip & 1:
        return core
    high = flip.bit_length() - 1
    return lax.rem(core + bit_of(me, high), 2)


def kernel(
    flip, grads, cover, cross, own, gains, rows, tiles, packed, landed, meta, meta_in,
    cover_in, load_sem, block_send, block_recv, tile_send, tile_recv, meta_send,
    meta_recv, cover_send, cover_recv,
):
    me = lax.axis_index("blk")
    other = partner_of(me, flip)
    gives = gives_of(me, flip)

    load = pltpu.make_async_copy(grads, rows.at[pl.ds(0, ROWS)], load_sem)
    load.start()
    barrier = pltpu.get_barrier_semaphore()
    pl.semaphore_signal(barrier, inc=1, device_id=(other,), device_id_type=MESH)
    pl.semaphore_wait(barrier, 1)

    def remote(src, dst, send, recv):
        return pltpu.make_async_remote_copy(
            src_ref=src, dst_ref=dst, send_sem=send, recv_sem=recv,
            device_id=(other,), device_id_type=MESH,
        )

    def stretch(c, start=0, size=STEP):
        return pl.ds(pl.multiple_of(start + c * size, size), size)

    def block_copy(c):
        return remote(
            grads.at[stretch(c)], rows.at[stretch(c, ROWS)], block_send.at[c], block_recv.at[c]
        )

    def tile_copy(c):
        return remote(
            packed.at[stretch(c)], landed.at[stretch(c)], tile_send.at[c], tile_recv.at[c]
        )

    def meta_copy(c):
        return remote(meta.at[c], meta_in.at[c], meta_send.at[c], meta_recv.at[c])

    def loop(count, body):
        lax.fori_loop(0, count, lambda i, carry: (body(i), carry)[1], 0)

    cover_copy = remote(cover, cover_in, cover_send, cover_recv)

    def normalize(at, count):
        def some(i):
            part = stretch(i, at, 16)
            values = rows[part].astype(jnp.float32)
            scale = 1.0 / jnp.sqrt(jnp.sum(values * values, axis=1, keepdims=True) + 1e-06)
            rows[part] = (values * scale).astype(jnp.bfloat16)

        loop(count // 16, some)

    def work(j):
        foreign = j >= PARTS
        c = j - PARTS

        @pl.when(foreign)
        def _():
            block_copy(c).wait_recv()
            normalize(j * STEP, STEP)

        def strip(n):
            tiles[stretch(j), stretch(n, 0, 256)] = lax.dot_general(
                rows[stretch(j)], rows[stretch(n, 0, 256)], (((1,), (1,)), ((), ())),
                preferred_element_type=jnp.float32,
            )

        loop(ROWS // 256, strip)

        @pl.when(foreign)
        def _():
            tile = tiles[stretch(j)]
            peak = jnp.max(jnp.abs(tile), axis=0, keepdims=True)
            inverse = jnp.where(peak > 0.0, 32767.0 / peak, 0.0)
            packed[stretch(c)] = jnp.round(tile * inverse).astype(jnp.int32).astype(jnp.int16)
            meta[c] = peak * (1.0 / 32767.0)
            tile_copy(c).start()
            meta_copy(c).start()

            def turn(k):
                flat = tiles[stretch(j), stretch(k, 0, 128)].T
                cross[stretch(k, 0, 128), stretch(c)] = flat
                mine = jnp.broadcast_to(cover[:, stretch(k, 0, 128)], (STEP, 128)).T
                gains[:, stretch(c)] += jnp.sum(
                    jnp.maximum(flat - mine, 0.0), axis=0, keepdims=True
                )
                theirs = jnp.broadcast_to(cover_in[:, stretch(c)], (128, STEP)).T
                meta[PARTS, :, stretch(k, 0, 128)] += jnp.sum(
                    jnp.maximum(tiles[stretch(j), stretch(k, 0, 128)] - theirs, 0.0),
                    axis=0, keepdims=True,
                )

            loop(ROWS // 128, turn)

    @pl.when(gives == 1)
    def _():
        cover_copy.start()
        loop(PARTS, lambda c: block_copy(c).start())

    gains[...] = jnp.zeros((1, ROWS), jnp.float32)
    meta[PARTS] = jnp.zeros((1, ROWS), jnp.float32)
    load.wait()
    normalize(0, ROWS)

    @pl.when(gives == 0)
    def _():
        cover_copy.wait_recv()

    loop(2 * PARTS - gives * PARTS, work)

    def settle(i):
        own[stretch(i)] = tiles[stretch(i)]

    loop(PARTS, settle)

    @pl.when(gives == 1)
    def _():
        def take(c):
            tile_copy(c).wait_recv()
            meta_copy(c).wait_recv()
            cross[stretch(c)] = landed[stretch(c)].astype(jnp.int32).astype(jnp.float32) * meta_in[c]

        loop(PARTS, take)
        meta_copy(PARTS).wait_recv()
        gains[...] = meta_in[PARTS]
        cover_copy.wait_send()
        loop(PARTS, lambda c: block_copy(c).wait_send())

    @pl.when(gives == 0)
    def _():
        meta_copy(PARTS).start()

        def sent(c):
            tile_copy(c).wait_send()
            meta_copy(c).wait_send()

        loop(PARTS, sent)
        meta_copy(PARTS).wait_send()


def paired(flip, grads, cover):
    dma = pltpu.SemaphoreType.DMA
    return pl.pallas_call(
        functools.partial(kernel, flip),
        out_shape=(
            jax.ShapeDtypeStruct((ROWS, ROWS), jnp.float32),
            jax.ShapeDtypeStruct((ROWS, ROWS), jnp.float32),
            jax.ShapeDtypeStruct((1, ROWS), jnp.float32),
        ),
        in_specs=[
            pl.BlockSpec(memory_space=pl.ANY),
            pl.BlockSpec(memory_space=pltpu.VMEM),
        ],
        out_specs=[pl.BlockSpec(memory_space=pltpu.VMEM)] * 3,
        scratch_shapes=[
            pltpu.VMEM((2 * ROWS, G), jnp.bfloat16),
            pltpu.VMEM((2 * ROWS, ROWS), jnp.float32),
            pltpu.VMEM((ROWS, ROWS), jnp.int16),
            pltpu.VMEM((ROWS, ROWS), jnp.int16),
            pltpu.VMEM((PARTS + 1, 1, ROWS), jnp.float32),
            pltpu.VMEM((PARTS + 1, 1, ROWS), jnp.float32),
            pltpu.VMEM((1, ROWS), jnp.float32),
            dma(()),
            dma((PARTS,)),
            dma((PARTS,)),
            dma((PARTS,)),
            dma((PARTS,)),
            dma((PARTS + 1,)),
            dma((PARTS + 1,)),
            dma(()),
            dma(()),
        ],
        compiler_params=pltpu.CompilerParams(
            collective_id=flip, has_side_effects=True, vmem_limit_bytes=32 << 20
        ),
        name="pair",
    )(grads, cover)


FUSED = (8, 24, 32, 43, 64, 91, 120, 146, 181, 200, 222, 255)


def product(left, right):
    return lax.dot_general(
        left, right, (((1,), (1,)), ((), ())), preferred_element_type=jnp.float32
    )


def unit_of(block):
    values = block.astype(jnp.float32)
    scale = 1.0 / jnp.sqrt(jnp.sum(values * values, axis=1, keepdims=True) + 1e-06)
    return (values * scale).astype(jnp.bfloat16)


def make(flips):
    def leaf(flip, grads, cover):
        if flip in FUSED:
            cross, own, gain = paired(flip, grads, cover[None])
            return cross, own, gain[0], grads
        zero = jnp.zeros((ROWS, ROWS), jnp.float32)
        block = lax.ppermute(grads, "blk", [(i, i ^ flip) for i in range(256)])
        return zero, zero, cover, block

    def choose(which, operands, lo, hi):
        if hi - lo == 1:
            return leaf(flips[lo], *operands)
        mid = (lo + hi) // 2
        return lax.cond(
            which < mid,
            lambda *o: choose(which, o, lo, mid),
            lambda *o: choose(which, o, mid, hi),
            *operands,
        )

    def shards(gradients, partner, cover):
        myself = lax.axis_index("blk")
        flip = jnp.bitwise_xor(partner[0], myself)
        cross, own, gain, block = choose(flip - 1, (gradients, cover), 0, len(flips))

        def rest():
            unit = unit_of(gradients)
            tile = product(unit, unit_of(block))
            return tile, product(unit, unit), jnp.sum(jnp.maximum(tile - cover[:, None], 0.0), axis=0)

        done = sum(jnp.where(flip == m, 1, 0) for m in FUSED) == 1
        return lax.cond(done, lambda: (cross, own, gain), rest)

    return shards


def solution(mesh):
    placed = (P("blk", None), P("blk"), P("blk"))
    return jax.shard_map(
        make(list(range(1, 256))),
        mesh=mesh,
        in_specs=placed,
        out_specs=(P("blk", None), P("blk", None), P("blk")),
        check_vma=False,
    )
```

```python
import functools

import jax
import jax.numpy as jnp
from jax import lax
from jax.experimental import pallas as pl
from jax.experimental.pallas import tpu as pltpu
from jax.sharding import PartitionSpec as P

MESH = pl.DeviceIdType.MESH


def opposite(me, flip):
    other = me
    for k in range(flip.bit_length()):
        if flip >> k & 1:
            other = other + (1 << k) * (1 - 2 * lax.rem(lax.div(me, 1 << k), 2))
    return other


def swap_kernel(flip, block, landed, send, receive):
    other = opposite(lax.axis_index("blk"), flip)
    barrier = pltpu.get_barrier_semaphore()
    pl.semaphore_signal(barrier, inc=1, device_id=(other,), device_id_type=MESH)
    pl.semaphore_wait(barrier, 1)
    copy = pltpu.make_async_remote_copy(
        src_ref=block, dst_ref=landed, send_sem=send, recv_sem=receive,
        device_id=(other,), device_id_type=MESH,
    )
    copy.start()
    copy.wait()


def swap(flip, block):
    return pl.pallas_call(
        functools.partial(swap_kernel, flip),
        out_shape=jax.ShapeDtypeStruct(block.shape, block.dtype),
        in_specs=[pl.BlockSpec(memory_space=pl.ANY)],
        out_specs=pl.BlockSpec(memory_space=pl.ANY),
        scratch_shapes=[pltpu.SemaphoreType.DMA, pltpu.SemaphoreType.DMA],
        compiler_params=pltpu.CompilerParams(collective_id=flip >> 1, has_side_effects=True),
        name="swap",
    )(block)


def chosen(which, block, low, high):
    if high - low == 1:
        return swap(2 * low, block) if low else block
    middle = (low + high) // 2
    return lax.cond(
        which < middle,
        lambda b: chosen(which, b, low, middle),
        lambda b: chosen(which, b, middle, high),
        block,
    )


def product(left, right):
    return lax.dot_general(
        left, right, (((1,), (1,)), ((), ())), preferred_element_type=jnp.float32
    )


def unit_of(block):
    values = block.astype(jnp.float32)
    scale = 1.0 / jnp.sqrt(jnp.sum(values * values, axis=1, keepdims=True) + 1e-06)
    return (values * scale).astype(jnp.bfloat16)


def make(flips=None):
    def shards(gradients, partner, cover):
        n = lax.axis_size("blk")
        flip = jnp.bitwise_xor(partner[0], lax.axis_index("blk"))
        landed = chosen(flip >> 1, gradients, 0, n // 2)
        crossed = lax.ppermute(landed, "blk", [(i, i ^ 1) for i in range(n)])
        unit = unit_of(gradients)
        own = product(unit, unit)
        other = unit_of(jnp.where(jnp.bitwise_and(flip, 1) == 1, crossed, landed))
        cross = product(unit, other)
        gain = jnp.sum(jnp.maximum(cross - cover[:, None], 0.0), axis=0)
        return (cross, own, gain)

    return shards


def solution(mesh):
    placed = (P("blk", None), P("blk"), P("blk"))
    return jax.shard_map(
        make(),
        mesh=mesh,
        in_specs=placed,
        out_specs=(P("blk", None), P("blk", None), P("blk")),
        check_vma=False,
    )
```

```python
import functools

import jax
import jax.numpy as jnp
from jax import lax
from jax.experimental import pallas as pl
from jax.experimental.pallas import tpu as pltpu
from jax.sharding import PartitionSpec as P

ROWS = 512
G = 2048
PIECE = ROWS // 2
MESH = pl.DeviceIdType.MESH


def opposite(me, flip):
    other = me
    for k in range(flip.bit_length()):
        if flip >> k & 1:
            other = other + (1 << k) * (1 - 2 * lax.rem(lax.div(me, 1 << k), 2))
    return other


def swap_kernel(flip, block, landed, send, receive):
    other = opposite(lax.axis_index("blk"), flip)
    barrier = pltpu.get_barrier_semaphore()
    pl.semaphore_signal(barrier, inc=1, device_id=(other,), device_id_type=MESH)
    pl.semaphore_wait(barrier, 1)
    copy = pltpu.make_async_remote_copy(
        src_ref=block, dst_ref=landed, send_sem=send, recv_sem=receive,
        device_id=(other,), device_id_type=MESH,
    )
    copy.start()
    copy.wait()


def swap(flip, block):
    return pl.pallas_call(
        functools.partial(swap_kernel, flip),
        out_shape=jax.ShapeDtypeStruct(block.shape, block.dtype),
        in_specs=[pl.BlockSpec(memory_space=pl.ANY)],
        out_specs=pl.BlockSpec(memory_space=pl.ANY),
        scratch_shapes=[pltpu.SemaphoreType.DMA, pltpu.SemaphoreType.DMA],
        compiler_params=pltpu.CompilerParams(collective_id=flip >> 1, has_side_effects=True),
        name="swap",
    )(block)


def chosen(which, block, low, high):
    if high - low == 1:
        return swap(2 * low, block) if low else block
    middle = (low + high) // 2
    return lax.cond(
        which < middle,
        lambda b: chosen(which, b, low, middle),
        lambda b: chosen(which, b, middle, high),
        block,
    )


def product(left, right):
    return lax.dot_general(
        left, right, (((1,), (1,)), ((), ())), preferred_element_type=jnp.float32
    )


def normalize(source, target):
    def some(i, carry):
        at = pl.ds(pl.multiple_of(i * 32, 32), 32)
        values = source[at].astype(jnp.float32)
        scale = 1.0 / jnp.sqrt(jnp.sum(values * values, axis=1, keepdims=True) + 1e-06)
        target[at] = (values * scale).astype(jnp.bfloat16)
        return carry

    lax.fori_loop(0, source.shape[0] // 32, some, 0, unroll=4)


def own_kernel(block, unit, own):
    normalize(block, unit)
    own[...] = product(unit[...], unit[...])


def cross_kernel(unit, block, cover, cross, gains, theirs):
    normalize(block, theirs)
    tile = product(unit[...], theirs[...])
    cross[...] = tile
    column = jnp.broadcast_to(cover[...], (128, ROWS)).T
    for i in range(PIECE // 128):
        at = slice(i * 128, (i + 1) * 128)
        gains[:, at] = jnp.sum(
            jnp.maximum(tile[:, at] - column, 0.0), axis=0, keepdims=True
        )


def both_kernel(mine, block, cover, own, cross, gains, unit, theirs):
    @pl.when(pl.program_id(0) == 0)
    def _():
        normalize(mine, unit)
        own[...] = product(unit[...], unit[...])

    cross_kernel(unit, block, cover, cross, gains, theirs)


def own_call(block):
    return pl.pallas_call(
        own_kernel,
        out_shape=(
            jax.ShapeDtypeStruct((ROWS, G), jnp.bfloat16),
            jax.ShapeDtypeStruct((ROWS, ROWS), jnp.float32),
        ),
        cost_estimate=pl.CostEstimate(
            flops=4 * ROWS * ROWS * G, bytes_accessed=8 << 20, transcendentals=0
        ),
        compiler_params=pltpu.CompilerParams(vmem_limit_bytes=24 << 20),
        name="own",
    )(block)


def cross_call(unit, block, cover):
    return pl.pallas_call(
        cross_kernel,
        grid=(ROWS // PIECE,),
        out_shape=(
            jax.ShapeDtypeStruct((ROWS, ROWS), jnp.float32),
            jax.ShapeDtypeStruct((1, ROWS), jnp.float32),
        ),
        in_specs=[
            pl.BlockSpec((ROWS, G), lambda i: (0, 0)),
            pl.BlockSpec((PIECE, G), lambda i: (i, 0)),
            pl.BlockSpec((1, ROWS), lambda i: (0, 0)),
        ],
        out_specs=[
            pl.BlockSpec((ROWS, PIECE), lambda i: (0, i)),
            pl.BlockSpec((1, PIECE), lambda i: (0, i)),
        ],
        scratch_shapes=[pltpu.VMEM((PIECE, G), jnp.bfloat16)],
        compiler_params=pltpu.CompilerParams(vmem_limit_bytes=24 << 20),
        name="cross",
    )(unit, block, cover)


def both_call(mine, block, cover):
    return pl.pallas_call(
        both_kernel,
        grid=(ROWS // PIECE,),
        out_shape=(
            jax.ShapeDtypeStruct((ROWS, ROWS), jnp.float32),
            jax.ShapeDtypeStruct((ROWS, ROWS), jnp.float32),
            jax.ShapeDtypeStruct((1, ROWS), jnp.float32),
        ),
        in_specs=[
            pl.BlockSpec((ROWS, G), lambda i: (0, 0)),
            pl.BlockSpec((PIECE, G), lambda i: (i, 0)),
            pl.BlockSpec((1, ROWS), lambda i: (0, 0)),
        ],
        out_specs=[
            pl.BlockSpec((ROWS, ROWS), lambda i: (0, 0)),
            pl.BlockSpec((ROWS, PIECE), lambda i: (0, i)),
            pl.BlockSpec((1, PIECE), lambda i: (0, i)),
        ],
        scratch_shapes=[
            pltpu.VMEM((ROWS, G), jnp.bfloat16),
            pltpu.VMEM((PIECE, G), jnp.bfloat16),
        ],
        compiler_params=pltpu.CompilerParams(vmem_limit_bytes=28 << 20),
        name="both",
    )(mine, block, cover)


def make(flips=None):
    def shards(gradients, partner, cover):
        n = lax.axis_size("blk")
        flip = jnp.bitwise_xor(partner[0], lax.axis_index("blk"))
        landed = chosen(flip >> 1, gradients, 0, n // 2)

        def turned():
            crossed = lax.ppermute(landed, "blk", [(i, i ^ 1) for i in range(n)])
            unit, own = own_call(gradients)
            return own, *cross_call(unit, crossed, cover[None])

        own, cross, gains = lax.cond(
            jnp.bitwise_and(flip, 1) == 1,
            turned,
            lambda: both_call(gradients, landed, cover[None]),
        )
        return (cross, own, gains[0])

    return shards


def solution(mesh):
    placed = (P("blk", None), P("blk"), P("blk"))
    return jax.shard_map(
        make(),
        mesh=mesh,
        in_specs=placed,
        out_specs=(P("blk", None), P("blk", None), P("blk")),
        check_vma=False,
    )
```
